32 devices in a mesh: seq: 16 (over z, y, core), tp: 2 (over x).
Axes of the slice: x: 2, y: 2, z: 4, core: 2. Of those that a mesh axis runs over, the one named last changes fastest.
Arguments:
- queries: bfloat16 [4096, 4096], P('seq', 'tp'), may hold values from -6 to 6, as said below
- keys: bfloat16 [4096, 512], P('seq', 'tp'), may hold values from -6 to 6, as said below
- values: bfloat16 [4096, 512], P('seq', 'tp'), may hold values from -6 to 6
- segment: int32 [4096], P('seq'), may hold values from 0 to 31, never falling along the last dimension, each value on 1 to 512 neighbouring positions
- repack: int32 [4096], P('seq'), may hold values from 0 to 4095, as said below
- proj: bfloat16 [1536, 4096], P('seq', 'tp'), may hold values from -0.5 to 0.5
- student_states: bfloat16 [4096, 1536], P('seq'), may hold values from -6 to 6
- target_row: int32 [4096], P('seq'), may hold values from 0 to 255
Outputs:
- student_rows: bfloat16 [4096, 1536], P('seq', 'tp')
- grad: float32 [1536, 4096], P('seq', 'tp')
The draws below stay inside these ranges and needn't reach their ends.
Inputs may be any that keep to these rules, and one draw needn't show every extreme that they name: `queries`: scaled normal entries. `keys`: scaled normal entries. `repack`: A permutation of the student rows. Each device's teacher rows go in consecutive groups of 32 rows, in order, each group to one student owner (the device holding student rows owner * 256 to owner * 256 + 255); every device sends exactly 32 rows to each of 8 other devices and none to itself, so at most 32 rows from one device to one owner, reached by every sending pair.
All inputs are finite; a program needn't handle non-finite values.
Results may differ from the reference program's by a relative error of at most 0.0056.
Values may be sent and summed in bfloat16 or wider, within the bound.
A program may use at most 64 MiB of HBM per device.

```python
import math
import jax
import jax.numpy as jnp
import numpy as np
from jax import lax

HEADS = 32
KV_HEADS = 4
HEAD_DIM = 128
SW = 1536
TOK_DEV = 256
REACH = 2
TOKENS = 4096
MOST_DOC = 512
DOCS = 32
CAP = 32


def draw_queries(key, part):
    base = jax.random.normal(jax.random.fold_in(key, 1), (TOKENS, HEADS, HEAD_DIM), jnp.float32)
    base = jnp.clip(base, -6.0, 6.0)
    return base.reshape(TOKENS, HEADS * HEAD_DIM).astype(jnp.bfloat16)


def draw_keys(key, part):
    base = jax.random.normal(jax.random.fold_in(key, 2), (TOKENS, KV_HEADS, HEAD_DIM), jnp.float32)
    base = jnp.clip(base, -6.0, 6.0)
    return base.reshape(TOKENS, KV_HEADS * HEAD_DIM).astype(jnp.bfloat16)


def draw_repack(key, part):
    groups = TOK_DEV // CAP
    senders = TOKENS // TOK_DEV
    offsets = jax.random.permutation(jax.random.fold_in(key, 11), senders - 1)[:groups] + 1

    def per_source(source):
        order = jax.random.permutation(jax.random.fold_in(jax.random.fold_in(key, 12), source), groups)
        owner = (source + offsets[order]) % senders
        group_rows = owner * TOK_DEV + order * CAP
        return (group_rows[:, None] + jnp.arange(CAP)[None, :]).reshape(-1)
    return jax.vmap(per_source)(jnp.arange(senders)).reshape(-1).astype(jnp.int32)


def plant(entries, stream_key, least, high):
    longest = entries.shape.index(max(entries.shape))
    spots = []
    for shift in (0, 1):
        where = [jax.random.randint(jax.random.fold_in(stream_key, axis), (), 0, length) for axis, length in enumerate(entries.shape)]
        where[longest] = (where[longest] + shift) % entries.shape[longest]
        spots.append(tuple(where))
    return entries.at[spots[0]].set(least).at[spots[1]].set(high)


def level_of(key, extent, shards, low, largest):
    def one(dim, shards_of):
        steps = jax.random.uniform(jax.random.fold_in(jax.random.fold_in(key, 6), dim), (shards_of,), jnp.float32, low / len(shards), largest / len(shards))
        return jnp.repeat(jnp.exp(steps), extent[dim] // shards_of).reshape((-1,) + (1,) * (len(extent) - dim - 1))

    factor_of = one(*shards[0])
    for cut in shards[1:]:
        factor_of = factor_of * one(*cut)
    return factor_of


def split_up(amount, total, limit, slope):
    portions = [(1 << 20) // math.isqrt(grade ** slope) + 1 for grade in range(2, amount + 1)]
    spare, counts = total - limit - (amount - 1), [1] * (amount - 1)
    while spare > 0:
        movable = [i for i in range(amount - 1) if counts[i] < limit]
        whole, remaining = sum([portions[i] for i in movable]), spare
        for i in movable:
            more = min(limit - counts[i], max(1, remaining * portions[i] // whole), spare)
            counts[i] = counts[i] + more
            spare = spare - more
    return np.array([limit] + counts)


def ragged_sizes(rng, count, total, reach, lean):
    if count == 2:
        one = jax.random.randint(rng, (), max(1, total - reach), min(reach, total - 1) + 1)
        return jnp.stack([one, total - one])
    lengths = jnp.asarray(split_up(count, total, reach, lean), jnp.int32)
    pairs = (count - 1) // 2
    donor, receiver = lengths[1:1 + 2 * pairs:2], lengths[2:2 + 2 * pairs:2]
    slack = jnp.minimum(donor - 1, reach - receiver)
    moved = jax.random.randint(jax.random.fold_in(rng, 1), (pairs,), 0, 1 << 20) % (slack + 1)
    lengths = lengths.at[1:1 + 2 * pairs:2].set(donor - moved).at[2:2 + 2 * pairs:2].set(receiver + moved)
    return lengths[jax.random.permutation(jax.random.fold_in(rng, 2), count)]


def gaussian(own_key, extent, spread, limit, cuts=(), held_as=jnp.bfloat16):
    level = level_of(own_key, extent, cuts, -0.22, 0.18) if cuts else 1.0
    result = jax.random.normal(own_key, extent, jnp.float32) * spread * level
    return jnp.minimum(jnp.maximum(result, -limit), limit).astype(held_as)


def setup_inputs(seed: int = 0) -> dict:
    splits = jax.random.split(jax.random.key(seed), 9)
    queries = draw_queries(jax.random.fold_in(splits[8], 71), 0)
    keys = draw_keys(jax.random.fold_in(splits[8], 71), 0)
    values = gaussian(splits[2], (TOKENS, KV_HEADS * HEAD_DIM), 1.0, 6.0, ((0, 16), (1, 2)))
    segment = jnp.searchsorted(jnp.cumsum(ragged_sizes(splits[3], DOCS, TOKENS, MOST_DOC, 2)), jnp.arange(TOKENS), side="right").astype(jnp.int32)
    repack = draw_repack(jax.random.fold_in(splits[8], 71), 0)
    proj = gaussian(splits[5], (SW, HEADS * HEAD_DIM), HEAD_DIM ** -0.5, 0.5, ((0, 16), (1, 2)))
    student_states = gaussian(splits[6], (TOKENS, SW), 1.0, 6.0, ((0, 16),))
    target_row = plant(jax.random.randint(splits[7], (TOKENS,), 0, TOK_DEV), jax.random.fold_in(splits[7], 1), 0, TOK_DEV - 1).astype(jnp.int32)
    return {"queries": queries, "keys": keys, "values": values, "segment": segment, "repack": repack, "proj": proj, "student_states": student_states, "target_row": target_row}


def document_attention(queries, keys, values, segment):
    group = HEADS // KV_HEADS
    pad_rows = REACH * TOK_DEV
    span = pad_rows + TOK_DEV
    keys_pad = jnp.concatenate([jnp.zeros((pad_rows, keys.shape[1]), keys.dtype), keys], 0)
    values_pad = jnp.concatenate([jnp.zeros((pad_rows, values.shape[1]), values.dtype), values], 0)
    segment_pad = jnp.concatenate([jnp.full((pad_rows,), -1, jnp.int32), segment.astype(jnp.int32)], 0)
    scale = 1.0 / math.sqrt(HEAD_DIM)

    def one_block(index):
        first = (index * TOK_DEV).astype(jnp.int32)
        query_rows = lax.dynamic_slice_in_dim(queries, first, TOK_DEV, 0)
        key_rows = lax.dynamic_slice_in_dim(keys_pad, first, span, 0)
        value_rows = lax.dynamic_slice_in_dim(values_pad, first, span, 0)
        query_seg = lax.dynamic_slice_in_dim(segment.astype(jnp.int32), first, TOK_DEV, 0)
        key_seg = lax.dynamic_slice_in_dim(segment_pad, first, span, 0)
        query_pos = first + jnp.arange(TOK_DEV, dtype=jnp.int32)
        key_pos = first - pad_rows + jnp.arange(span, dtype=jnp.int32)
        allowed = (query_seg[:, None] == key_seg[None, :]) & (key_pos[None, :] <= query_pos[:, None])
        q_heads = query_rows.reshape(TOK_DEV, KV_HEADS, group, HEAD_DIM).astype(jnp.float32)
        k_heads = key_rows.reshape(span, KV_HEADS, HEAD_DIM).astype(jnp.float32)
        v_heads = value_rows.reshape(span, KV_HEADS, HEAD_DIM).astype(jnp.float32)
        scores = jnp.einsum('tgjd,sgd->gjts', q_heads, k_heads) * scale
        scores = jnp.where(allowed[None, None], scores, -1e+30)
        top = lax.optimization_barrier(jnp.max(scores, axis=-1, keepdims=True))
        expo = jnp.exp(scores - top)
        weights = (expo / lax.optimization_barrier(jnp.sum(expo, axis=-1, keepdims=True))).astype(jnp.bfloat16)
        mixed = jnp.einsum('gjts,sgd->tgjd', weights.astype(jnp.float32), v_heads)
        return mixed.reshape(TOK_DEV, HEADS * HEAD_DIM).astype(jnp.bfloat16)
    blocks = lax.map(one_block, jnp.arange(TOKENS // TOK_DEV, dtype=jnp.int32))
    return blocks.reshape(TOKENS, HEADS * HEAD_DIM)

def reference(queries, keys, values, segment, repack, proj, student_states, target_row):
    attended = document_attention(queries, keys, values, segment)
    moved = jnp.zeros_like(attended).at[repack.astype(jnp.int32)].set(attended)
    student_full = jnp.dot(moved, proj.T, preferred_element_type=jnp.float32)
    student_rows = student_full.astype(jnp.bfloat16)
    base_row = jnp.arange(TOKENS, dtype=jnp.int32) // TOK_DEV * TOK_DEV
    target = student_states[base_row + target_row.astype(jnp.int32)]
    delta = (student_rows.astype(jnp.float32) - target.astype(jnp.float32)).astype(jnp.bfloat16)
    grad = jnp.dot(delta.T, moved, preferred_element_type=jnp.float32) * (1.0 / math.sqrt(TOKENS))
    return (student_rows, grad)
```

```python
import functools
import math

import jax
import jax.numpy as jnp
from jax import lax
from jax.experimental import pallas as pl
from jax.experimental.pallas import tpu as pltpu
from jax.sharding import PartitionSpec as P

HEADS = 32
KV_HEADS = 4
HEAD_DIM = 128
SW = 1536
REACH = 2

neg_large = -1e30


def attention_kernel(q_ref, *refs):
    blocks = REACH + 1
    k_refs, v_refs = refs[:blocks], refs[blocks : 2 * blocks]
    seg_q_ref, seg_k_ref, out_ref, bias = refs[2 * blocks :]
    rows = q_ref.shape[0]
    before = REACH * rows

    @pl.when(pl.program_id(0) == 0)
    def _():
        q_pos = lax.broadcasted_iota(jnp.int32, bias.shape, 0) + before
        k_pos = lax.broadcasted_iota(jnp.int32, bias.shape, 1)
        allowed = (seg_q_ref[...] == seg_k_ref[...]) & (k_pos <= q_pos)
        bias[...] = jnp.where(allowed, 0.0, neg_large)

    scale = math.log2(math.e) / math.sqrt(HEAD_DIM)
    keys = jnp.concatenate([ref[...] for ref in k_refs], axis=0)
    values = jnp.concatenate([ref[...] for ref in v_refs], axis=0)
    scores = lax.dot_general(
        q_ref[...], keys, (((1,), (1,)), ((), ())), preferred_element_type=jnp.float32
    )
    scores = scores * scale + bias[...]
    top = jnp.max(scores, axis=-1, keepdims=True)
    expo = jnp.exp2(scores - top)
    total = jnp.sum(expo, axis=-1, keepdims=True)
    mixed = jnp.dot(expo.astype(jnp.bfloat16), values, preferred_element_type=jnp.float32)
    out_ref[...] = (mixed / total).astype(out_ref.dtype)


def attend(queries, key_list, value_list, seg_q, seg_k):
    rows, width = queries.shape
    group = HEADS // KV_HEADS
    head_spec = pl.BlockSpec((rows, HEAD_DIM), lambda h: (0, h))
    kv_spec = pl.BlockSpec((rows, HEAD_DIM), lambda h: (0, h // group))
    span = seg_k.shape[1]
    heads = width // HEAD_DIM
    return pl.pallas_call(
        attention_kernel,
        grid=(heads,),
        out_shape=jax.ShapeDtypeStruct(queries.shape, jnp.bfloat16),
        in_specs=[head_spec]
        + [kv_spec] * (2 * (REACH + 1))
        + [
            pl.BlockSpec((rows, 1), lambda h: (0, 0)),
            pl.BlockSpec((1, span), lambda h: (0, 0)),
        ],
        out_specs=head_spec,
        scratch_shapes=[pltpu.VMEM((rows, span), jnp.float32)],
        compiler_params=pltpu.CompilerParams(
            dimension_semantics=("arbitrary",), vmem_limit_bytes=24 * 1024 * 1024
        ),
        cost_estimate=pl.CostEstimate(
            flops=4 * heads * rows * span * HEAD_DIM,
            bytes_accessed=6 * rows * width,
            transcendentals=heads * rows * span,
        ),
    )(queries, *key_list, *value_list, seg_q, seg_k)


def bf16_dot(a, b, contract):
    return lax.dot_general(a, b, (contract, ((), ())), preferred_element_type=jnp.float32)


def select(mask, rows):
    return jnp.dot(
        mask.astype(jnp.bfloat16), rows, preferred_element_type=jnp.float32
    ).astype(jnp.bfloat16)


def on_device(queries, keys, values, segment, repack, proj, student_states, target_row):
    bf16 = jnp.bfloat16
    row_count = queries.shape[0]
    devices, tp_size = lax.axis_size("seq"), lax.axis_size("tp")
    here, tp_index = lax.axis_index("seq"), lax.axis_index("tp")
    core = lax.rem(here, 2)
    chips = devices // 2
    same_core = [[2 * k + c for k in range(chips)] for c in range(2)]
    swap = [(i, i ^ 1) for i in range(devices)]
    capacity = max(2 * row_count // devices, 2)
    groups = row_count // capacity
    share = SW // tp_size
    half = share // 2
    piece = proj.shape[0]
    features = proj.shape[1]

    def to_partner(block):
        return lax.ppermute(block, "seq", swap)

    table = lax.all_gather(jnp.stack([segment, repack]), "seq", axis=0)
    whole_proj = lax.all_gather(proj, "seq", axis=0, tiled=True, axis_index_groups=same_core)

    key_list, value_list = [keys], [values]
    for step in range(1, REACH + 1):
        route = [(i - step, i) for i in range(step, devices)]
        earlier_k, earlier_v = lax.ppermute((keys, values), "seq", route)
        key_list.insert(0, earlier_k)
        value_list.insert(0, earlier_v)
    seg_list = []
    for step in range(REACH, 0, -1):
        earlier = lax.dynamic_index_in_dim(table, jnp.maximum(here - step, 0), 0, False)[0]
        seg_list.append(jnp.where(here >= step, earlier, -1))
    seg_k = jnp.concatenate(seg_list + [segment])[None, :]

    repack_all = table[:, 1]
    owner_all = repack_all // row_count
    mine = (owner_all == here).reshape(devices, groups, capacity)
    local = (repack_all - here * row_count).reshape(devices, groups, capacity)
    slots = jnp.max(jnp.where(mine, local, -1), axis=1).reshape(-1)
    row_ids = jnp.arange(row_count, dtype=jnp.int32)
    bucket = (repack // row_count) * capacity + row_ids % capacity
    bucket_ids = jnp.arange(devices * capacity, dtype=jnp.int32)

    blocks = half // piece
    states = lax.dynamic_slice_in_dim(student_states, tp_index * share, share, 1)
    states = states.reshape(row_count, blocks, 2, piece).transpose(0, 2, 1, 3)
    states = states.reshape(row_count, share)
    targets = select(target_row[:, None] == row_ids[None, :], states)
    outgoing = select(slots[:, None] == row_ids[None, :], targets)
    incoming = lax.all_to_all(
        outgoing.reshape(devices, capacity, share), "seq", split_axis=0, concat_axis=0, tiled=True
    ).reshape(devices * capacity, share)
    own_target = select(bucket[:, None] == bucket_ids[None, :], incoming)
    even, odd = own_target[:, :half], own_target[:, half:]
    target_keep = jnp.where(core == 0, even, odd)
    target_give = jnp.where(core == 0, odd, even)
    target = jnp.concatenate([target_keep, to_partner(target_give)], axis=0)

    attended = attend(queries, key_list, value_list, segment[:, None], seg_k)
    both = jnp.concatenate([attended, to_partner(attended)], axis=0)

    y_part = bf16_dot(both, whole_proj, ((1,), (1,)))
    y_sum = lax.dynamic_slice_in_dim(y_part, tp_index * half, half, 1)
    for shift in range(1, tp_size):
        route = [(i, (i + shift) % tp_size) for i in range(tp_size)]
        to = lax.rem(tp_index + shift, tp_size)
        give = lax.dynamic_slice_in_dim(y_part, to * half, half, 1).astype(bf16)
        y_sum = y_sum + lax.ppermute(give, "tp", route).astype(jnp.float32)
    y_share = y_sum.astype(bf16)
    delta_share = (y_share.astype(jnp.float32) - target.astype(jnp.float32)).astype(bf16)
    delta = lax.all_gather(delta_share, "tp", axis=1, tiled=True)

    y_own, y_other = y_share[:row_count], to_partner(y_share[row_count:])
    y_even = jnp.where(core == 0, y_own, y_other).reshape(row_count, blocks, 1, piece)
    y_odd = jnp.where(core == 0, y_other, y_own).reshape(row_count, blocks, 1, piece)
    y_rows = jnp.concatenate([y_even, y_odd], axis=2).reshape(row_count, share)
    buckets = select(bucket_ids[:, None] == bucket[None, :], y_rows)
    arrived = lax.all_to_all(
        buckets.reshape(devices, capacity, share), "seq", split_axis=0, concat_axis=0, tiled=True
    ).reshape(devices * capacity, share)
    out_rows = select(row_ids[:, None] == slots[None, :], arrived)

    term = bf16_dot(delta, both, ((0,), (0,)))
    summed = lax.psum_scatter(
        term.astype(bf16).reshape(chips * piece, features),
        "seq",
        scatter_dimension=0,
        tiled=True,
        axis_index_groups=same_core,
    )
    grad = summed.astype(jnp.float32) * (1.0 / math.sqrt(row_count * devices))
    return (out_rows, grad)


def solution(mesh):
    placed = (
        P("seq", "tp"),
        P("seq", "tp"),
        P("seq", "tp"),
        P("seq"),
        P("seq"),
        P("seq", "tp"),
        P("seq", None),
        P("seq"),
    )
    return jax.shard_map(
        on_device,
        mesh=mesh,
        in_specs=placed,
        out_specs=(P("seq", "tp"), P("seq", "tp")),
        check_vma=False,
    )
```

```python
import functools
import math

import jax
import jax.numpy as jnp
from jax import lax
from jax.experimental import pallas as pl
from jax.experimental.pallas import tpu as pltpu
from jax.sharding import PartitionSpec as P

HEADS = 32
KV_HEADS = 4
HEAD_DIM = 128
SW = 1536
REACH = 2

neg_large = -1e30


def attention_kernel(q_ref, *refs):
    blocks = REACH + 1
    k_refs, v_refs = refs[:blocks], refs[blocks : 2 * blocks]
    seg_q_ref, seg_k_ref, out_ref, bias = refs[2 * blocks :]
    rows = q_ref.shape[0]
    before = REACH * rows

    @pl.when(pl.program_id(0) == 0)
    def _():
        q_pos = lax.broadcasted_iota(jnp.int32, bias.shape, 0) + before
        k_pos = lax.broadcasted_iota(jnp.int32, bias.shape, 1)
        allowed = (seg_q_ref[...] == seg_k_ref[...]) & (k_pos <= q_pos)
        bias[...] = jnp.where(allowed, 0.0, neg_large)

    scale = math.log2(math.e) / math.sqrt(HEAD_DIM)
    keys = jnp.concatenate([ref[...] for ref in k_refs], axis=0)
    values = jnp.concatenate([ref[...] for ref in v_refs], axis=0)
    scores = lax.dot_general(
        q_ref[...], keys, (((1,), (1,)), ((), ())), preferred_element_type=jnp.float32
    )
    scores = scores * scale + bias[...]
    top = jnp.max(scores, axis=-1, keepdims=True)
    expo = jnp.exp2(scores - top)
    total = jnp.sum(expo, axis=-1, keepdims=True)
    mixed = jnp.dot(expo.astype(jnp.bfloat16), values, preferred_element_type=jnp.float32)
    out_ref[...] = (mixed / total).astype(out_ref.dtype)


def attend(queries, key_list, value_list, seg_q, seg_k):
    rows, width = queries.shape
    group = HEADS // KV_HEADS
    head_spec = pl.BlockSpec((rows, HEAD_DIM), lambda h: (0, h))
    kv_spec = pl.BlockSpec((rows, HEAD_DIM), lambda h: (0, h // group))
    span = seg_k.shape[1]
    heads = width // HEAD_DIM
    return pl.pallas_call(
        attention_kernel,
        grid=(heads,),
        out_shape=jax.ShapeDtypeStruct(queries.shape, jnp.bfloat16),
        in_specs=[head_spec]
        + [kv_spec] * (2 * (REACH + 1))
        + [
            pl.BlockSpec((rows, 1), lambda h: (0, 0)),
            pl.BlockSpec((1, span), lambda h: (0, 0)),
        ],
        out_specs=head_spec,
        scratch_shapes=[pltpu.VMEM((rows, span), jnp.float32)],
        compiler_params=pltpu.CompilerParams(
            dimension_semantics=("arbitrary",), vmem_limit_bytes=24 * 1024 * 1024
        ),
        cost_estimate=pl.CostEstimate(
            flops=4 * heads * rows * span * HEAD_DIM,
            bytes_accessed=6 * rows * width,
            transcendentals=heads * rows * span,
        ),
    )(queries, *key_list, *value_list, seg_q, seg_k)


def bf16_dot(a, b, contract):
    return lax.dot_general(a, b, (contract, ((), ())), preferred_element_type=jnp.float32)


def select(mask, rows):
    return jnp.dot(
        mask.astype(jnp.bfloat16), rows, preferred_element_type=jnp.float32
    ).astype(jnp.bfloat16)


def scatter_kernel(seq_size, delta_ref, rows_ref, out_ref, *scratch):
    send_y, recv_y, send_r, recv_r, send_l, recv_l, sem_y, sem_r, sem_l = scratch
    here, tp_index = lax.axis_index("seq"), lax.axis_index("tp")
    line = seq_size // 4
    core = here % 2
    y = (here // 2) % 2
    z = here // 4
    piece = out_ref.shape[0]

    def device(z_to, y_to):
        return ((z_to * 2 + y_to) * 2 + core, tp_index)

    def copy(src, dst, sems, slot, to):
        return pltpu.make_async_remote_copy(
            src_ref=src.at[slot],
            dst_ref=dst.at[slot],
            send_sem=sems.at[0, slot],
            recv_sem=sems.at[1, slot],
            device_id=to,
            device_id_type=pl.DeviceIdType.MESH,
        )

    def to_y(slot):
        return copy(send_y, recv_y, sem_y, slot, device(z, 1 - y))

    def to_right(slot):
        return copy(send_r, recv_r, sem_r, slot, device((z + 1) % line, y))

    def to_left(slot):
        return copy(send_l, recv_l, sem_l, slot, device((z + line - 1) % line, y))

    def term(z_of, y_of):
        first = pl.multiple_of((z_of * 2 + y_of) * piece, piece)
        return jnp.dot(
            delta_ref[pl.ds(first, piece), :], rows_ref[...], preferred_element_type=jnp.float32
        )

    has_left, has_right = z > 0, z < line - 1
    barrier = pltpu.get_barrier_semaphore()

    def greet(to):
        pl.semaphore_signal(barrier, inc=1, device_id=to, device_id_type=pl.DeviceIdType.MESH)

    greet(device(z, 1 - y))
    pl.when(has_left)(lambda: greet(device(z - 1, y)))
    pl.when(has_right)(lambda: greet(device(z + 1, y)))
    peers = 1 + has_left.astype(jnp.int32) + has_right.astype(jnp.int32)
    pl.semaphore_wait(barrier, peers)

    def start_y(slot):
        send_y[slot] = term(slot, 1 - y).astype(jnp.bfloat16)
        to_y(slot).start()

    def summed(slot):
        own = term(slot, y)
        to_y(slot).wait_recv()
        return own + recv_y[slot].astype(jnp.float32)

    def pass_right(slot):
        send_r[slot] = summed(slot).astype(jnp.bfloat16)

        @pl.when(has_left)
        def _():
            to_right(slot).wait_recv()
            added = send_r[slot].astype(jnp.float32) + recv_r[slot].astype(jnp.float32)
            send_r[slot] = added.astype(jnp.bfloat16)

        to_right(slot).start()

    def pass_left(slot):
        send_l[slot] = summed(slot).astype(jnp.bfloat16)

        @pl.when(has_right)
        def _():
            to_left(slot).wait_recv()
            added = send_l[slot].astype(jnp.float32) + recv_l[slot].astype(jnp.float32)
            send_l[slot] = added.astype(jnp.bfloat16)

        to_left(slot).start()

    def farthest_first(right, left):
        for distance in range(line - 1, 0, -1):
            pl.when(z + distance < line)(lambda: right(z + distance))
            pl.when(z - distance >= 0)(lambda: left(z - distance))

    farthest_first(start_y, start_y)
    start_y(z)
    farthest_first(pass_right, pass_left)
    out_ref[...] = summed(z)

    @pl.when(has_left)
    def _():
        to_right(z).wait_recv()
        out_ref[...] += recv_r[z].astype(jnp.float32)

    @pl.when(has_right)
    def _():
        to_left(z).wait_recv()
        out_ref[...] += recv_l[z].astype(jnp.float32)

    for slot in range(line):
        to_y(slot).wait_send()
    farthest_first(lambda slot: to_right(slot).wait_send(), lambda slot: to_left(slot).wait_send())


def scatter_terms(delta_rows, rows, seq_size):
    line = seq_size // 4
    piece, width = delta_rows.shape[0] // (seq_size // 2), rows.shape[1]
    return pl.pallas_call(
        functools.partial(scatter_kernel, seq_size),
        out_shape=jax.ShapeDtypeStruct((piece, width), jnp.float32),
        in_specs=[pl.BlockSpec(memory_space=pltpu.VMEM)] * 2,
        out_specs=pl.BlockSpec(memory_space=pltpu.VMEM),
        scratch_shapes=[pltpu.VMEM((line, piece, width), jnp.bfloat16)] * 6
        + [pltpu.SemaphoreType.DMA((2, line))] * 3,
        compiler_params=pltpu.CompilerParams(
            collective_id=0, has_side_effects=True, vmem_limit_bytes=40 * 1024 * 1024
        ),
        cost_estimate=pl.CostEstimate(
            flops=2 * delta_rows.size * width, bytes_accessed=rows.size * 2, transcendentals=0
        ),
    )(delta_rows, rows)


def on_device(queries, keys, values, segment, repack, proj, student_states, target_row):
    bf16 = jnp.bfloat16
    row_count = queries.shape[0]
    devices, tp_size = lax.axis_size("seq"), lax.axis_size("tp")
    here, tp_index = lax.axis_index("seq"), lax.axis_index("tp")
    core = lax.rem(here, 2)
    chips = devices // 2
    same_core = [[2 * k + c for k in range(chips)] for c in range(2)]
    swap = [(i, i ^ 1) for i in range(devices)]
    capacity = max(2 * row_count // devices, 2)
    groups = row_count // capacity
    share = SW // tp_size
    half = share // 2
    piece = proj.shape[0]
    features = proj.shape[1]

    def to_partner(block):
        return lax.ppermute(block, "seq", swap)

    table = lax.all_gather(jnp.stack([segment, repack]), "seq", axis=0)
    whole_proj = lax.all_gather(proj, "seq", axis=0, tiled=True, axis_index_groups=same_core)

    key_list, value_list = [keys], [values]
    for step in range(1, REACH + 1):
        route = [(i - step, i) for i in range(step, devices)]
        earlier_k, earlier_v = lax.ppermute((keys, values), "seq", route)
        key_list.insert(0, earlier_k)
        value_list.insert(0, earlier_v)
    seg_list = []
    for step in range(REACH, 0, -1):
        earlier = lax.dynamic_index_in_dim(table, jnp.maximum(here - step, 0), 0, False)[0]
        seg_list.append(jnp.where(here >= step, earlier, -1))
    seg_k = jnp.concatenate(seg_list + [segment])[None, :]

    repack_all = table[:, 1]
    owner_all = repack_all // row_count
    mine = (owner_all == here).reshape(devices, groups, capacity)
    local = (repack_all - here * row_count).reshape(devices, groups, capacity)
    slots = jnp.max(jnp.where(mine, local, -1), axis=1).reshape(-1)
    row_ids = jnp.arange(row_count, dtype=jnp.int32)
    bucket = (repack // row_count) * capacity + row_ids % capacity
    bucket_ids = jnp.arange(devices * capacity, dtype=jnp.int32)

    blocks = half // piece
    states = lax.dynamic_slice_in_dim(student_states, tp_index * share, share, 1)
    states = states.reshape(row_count, blocks, 2, piece).transpose(0, 2, 1, 3)
    states = states.reshape(row_count, share)
    targets = select(target_row[:, None] == row_ids[None, :], states)
    outgoing = select(slots[:, None] == row_ids[None, :], targets)
    incoming = lax.all_to_all(
        outgoing.reshape(devices, capacity, share), "seq", split_axis=0, concat_axis=0, tiled=True
    ).reshape(devices * capacity, share)
    own_target = select(bucket[:, None] == bucket_ids[None, :], incoming)
    even, odd = own_target[:, :half], own_target[:, half:]
    target_keep = jnp.where(core == 0, even, odd)
    target_give = jnp.where(core == 0, odd, even)
    target = jnp.concatenate([target_keep, to_partner(target_give)], axis=0)

    attended = attend(queries, key_list, value_list, segment[:, None], seg_k)
    both = jnp.concatenate([attended, to_partner(attended)], axis=0)

    y_part = bf16_dot(both, whole_proj, ((1,), (1,)))
    y_sum = lax.dynamic_slice_in_dim(y_part, tp_index * half, half, 1)
    for shift in range(1, tp_size):
        route = [(i, (i + shift) % tp_size) for i in range(tp_size)]
        to = lax.rem(tp_index + shift, tp_size)
        give = lax.dynamic_slice_in_dim(y_part, to * half, half, 1).astype(bf16)
        y_sum = y_sum + lax.ppermute(give, "tp", route).astype(jnp.float32)
    y_share = y_sum.astype(bf16)
    delta_share = (y_share.astype(jnp.float32) - target.astype(jnp.float32)).astype(bf16)
    delta = lax.all_gather(delta_share, "tp", axis=1, tiled=True)

    y_own, y_other = y_share[:row_count], to_partner(y_share[row_count:])
    y_even = jnp.where(core == 0, y_own, y_other).reshape(row_count, blocks, 1, piece)
    y_odd = jnp.where(core == 0, y_other, y_own).reshape(row_count, blocks, 1, piece)
    y_rows = jnp.concatenate([y_even, y_odd], axis=2).reshape(row_count, share)
    buckets = select(bucket_ids[:, None] == bucket[None, :], y_rows)
    arrived = lax.all_to_all(
        buckets.reshape(devices, capacity, share), "seq", split_axis=0, concat_axis=0, tiled=True
    ).reshape(devices * capacity, share)
    out_rows = select(row_ids[:, None] == slots[None, :], arrived)

    if devices % 4 == 0 and devices <= 32 and piece % 16 == 0:
        summed = scatter_terms(delta.T, both, devices)
    else:
        term = bf16_dot(delta, both, ((0,), (0,)))
        summed = lax.psum_scatter(
            term.astype(bf16).reshape(chips * piece, features),
            "seq",
            scatter_dimension=0,
            tiled=True,
            axis_index_groups=same_core,
        ).astype(jnp.float32)
    grad = summed * (1.0 / math.sqrt(row_count * devices))
    return (out_rows, grad)


def solution(mesh):
    placed = (
        P("seq", "tp"),
        P("seq", "tp"),
        P("seq", "tp"),
        P("seq"),
        P("seq"),
        P("seq", "tp"),
        P("seq", None),
        P("seq"),
    )
    return jax.shard_map(
        on_device,
        mesh=mesh,
        in_specs=placed,
        out_specs=(P("seq", "tp"), P("seq", "tp")),
        check_vma=False,
    )
```
